32 devices in a mesh: dp: 8 (over z, x), tensor: 4 (over y, core).
Axes of the slice: x: 2, y: 2, z: 4, core: 2. Of those that a mesh axis runs over, the one named last changes fastest.
Arguments:
- grads: bfloat16 [8, 1024, 12288], P('dp', 'tensor'), may hold values from -65 to 65
- errors: bfloat16 [8, 1024, 12288], P('dp', 'tensor'), may hold values from -4 to 4
- q_init: float32 [4, 12288], replicated, may hold values from -6 to 6
- bias_grads: float32 [8, 12288], P('dp', 'tensor'), may hold values from -6 to 6
- head_group: int32 [96, 1], replicated, may hold values from 0 to 7
Outputs:
- new_errors: bfloat16 [8, 1024, 12288], P('dp', 'tensor')
- p_factor: float32 [4, 1024], P(None, 'tensor')
- q_factor: float32 [4, 12288], replicated
- bias_update: float32 [1024], P('tensor')
The draws below stay inside these ranges and needn't reach their ends.
Inputs may be any that keep to these rules, and one draw needn't show every extreme that they name: `head_group`: every group is named by at least one query head.
All inputs are finite; a program needn't handle non-finite values.
Results may differ from the reference program's by a relative error of at most 0.001.
Values sent between devices are 32-bit elements; how exact they have to be, the bound alone decides.
No kernel may reach another device: no remote copies, remote signals or barrier semaphores. Data moves between devices by JAX's collectives and lax.ppermute only.
A program may use at most 64 MiB of HBM per device.

```python
import math
import jax
import jax.numpy as jnp
from jax import lax

D = 12288
QH = 96
HD = 128
NG = 8
RANK = 4
KV = 1024
N_DP = 8


def draw_grads(key, part):
    key = jax.random.fold_in(key, 11)
    key_main, key_rows, key_cols = jax.random.split(key, 3)
    position = jnp.arange(KV, dtype=jnp.float32) / KV
    row_scale = jnp.exp(position * math.log(3.0)) * jnp.exp(jax.random.uniform(key_rows, (KV,)) * math.log(4.0))
    col_scale = jnp.exp(jax.random.uniform(key_cols, (D,)) * math.log(3.0))
    noise = jax.random.normal(key_main, (N_DP, KV, D))
    noise = jnp.clip(noise, -6.0, 6.0)
    values = 0.3 * noise * row_scale[None, :, None] * col_scale[None, None, :]
    return values.astype(jnp.bfloat16)


def shard_levels(key, shape, pieces, low, largest):
    loudness, own = 1.0, jax.random.fold_in(key, 6)
    for dim, blocks in pieces:
        steps = jnp.exp(jax.random.uniform(jax.random.fold_in(own, dim), (blocks,), jnp.float32, low / len(pieces), largest / len(pieces)))
        loudness = loudness * jnp.repeat(steps, shape[dim] // blocks).reshape([-1 if axis == dim else 1 for axis in range(len(shape))])
    return loudness


def choose_distinct(own_key, rows, number_of, top, lift):
    ranking = jax.random.permutation(jax.random.fold_in(own_key, 1), number_of)
    favour = ranking
    for power in range(3):
        favour = favour * favour // number_of
    favour = favour * lift // number_of
    tickets = jax.random.randint(jax.random.fold_in(own_key, 2), (rows, number_of), 0, 4096) + favour
    sure = jax.random.permutation(jax.random.fold_in(own_key, 3), rows)[jnp.arange(number_of) % rows]
    tickets = jnp.where(jnp.arange(rows)[:, None] == sure[None, :], 1 << 14, tickets)
    merit = tickets * number_of + jnp.arange(number_of)
    return lax.top_k(merit.astype(jnp.int32), top)[1].astype(jnp.int32)


def gaussian(own_key, dims, scale, bound, cuts=(), kind=jnp.bfloat16):
    factor_of = shard_levels(own_key, dims, cuts, -0.22, 0.18) if cuts else 1.0
    entries = jax.random.normal(own_key, dims, jnp.float32) * scale * factor_of
    return jnp.minimum(jnp.maximum(entries, -bound), bound).astype(kind)


def setup_inputs(seed: int = 0) -> dict:
    arg_keys = jax.random.split(jax.random.key(seed), 6)
    return {
        "grads": draw_grads(jax.random.fold_in(arg_keys[5], 71), 0),
        "errors": gaussian(arg_keys[1], (N_DP, KV, D), 0.3, 4.0, ((0, 8), (1, 4))),
        "q_init": gaussian(arg_keys[2], (RANK, D), 1.0, 6.0, (), jnp.float32),
        "bias_grads": gaussian(arg_keys[3], (N_DP, QH * HD), 1.0, 6.0, ((0, 8), (1, 4)), jnp.float32),
        "head_group": choose_distinct(arg_keys[4], QH, NG, 1, 1024),
    }


def reference(grads, errors, q_init, bias_grads, head_group):
    highest = lax.Precision.HIGHEST

    def merge_one(index):
        return grads[index].astype(jnp.float32) + errors[index].astype(jnp.float32)

    def left_step(carry, index):
        merged = merge_one(index)
        return (carry + jnp.dot(merged, q_init.T, precision=highest), None)
    left_sum, _ = lax.scan(left_step, jnp.zeros((KV, RANK), jnp.float32), jnp.arange(N_DP, dtype=jnp.int32))
    left = left_sum / N_DP
    gram_matrix = jnp.dot(left.T, left, precision=highest)
    chol_lower = jnp.linalg.cholesky(gram_matrix)
    p_factor = jax.scipy.linalg.solve_triangular(chol_lower, left.T, lower=True)

    def right_step(carry, index):
        merged = merge_one(index)
        return (carry + jnp.dot(p_factor, merged, precision=highest), None)
    right_sum, _ = lax.scan(right_step, jnp.zeros((RANK, D), jnp.float32), jnp.arange(N_DP, dtype=jnp.int32))
    q_factor = right_sum / N_DP
    approx = jnp.dot(p_factor.T, q_factor, precision=highest)

    def error_one(index):
        return (merge_one(index) - approx).astype(jnp.bfloat16)
    new_errors = lax.map(error_one, jnp.arange(N_DP, dtype=jnp.int32))
    groups = head_group[:, 0]
    onehot = (groups[None, :] == jnp.arange(NG, dtype=jnp.int32)[:, None]).astype(jnp.float32)
    counts = jnp.sum(onehot, axis=1)
    summed_bias = jnp.sum(bias_grads, axis=0).reshape(QH, HD)
    pooled = jnp.dot(onehot, summed_bias, precision=highest) / (counts[:, None] * N_DP)
    bias_update = pooled.reshape(KV)
    return (new_errors, p_factor, q_factor, bias_update)
```

```python
import functools
import math

import jax
import jax.numpy as jnp
from jax import lax
from jax.experimental import pallas as pl
from jax.experimental.pallas import tpu as pltpu
from jax.sharding import PartitionSpec as P

HD = 128
NG = 8
RANK = 4
LANES = 128
MIB = 1 << 20
F32 = jnp.float32
BF16 = jnp.bfloat16


def split3(x):
    high = x.astype(BF16).astype(F32)
    rest = x - high
    mid = rest.astype(BF16).astype(F32)
    return high, mid, rest - mid


def stack16(x):
    high, mid, low = split3(x)
    return jnp.concatenate([high, mid, low, jnp.zeros_like(x)], axis=0).astype(BF16)


def fold16(x):
    return (x[8:12] + x[4:8]) + x[0:4]


def butterfly_sum(parts):
    while len(parts) > 1:
        parts = [parts[i] + parts[i + 1] for i in range(0, len(parts), 2)]
    return parts[0]


def left_kernel(block, replicas, groups_hbm, q_hbm, bias_hbm, grads_hbm, errors_hbm, left_ref, bias_out, grads_ref, errors_ref, groups_ref, q_ref, q16_ref, wide_q, bias_ref, sums_ref, small_sems, sems):
    rows, width = grads_hbm.shape
    strip = 32
    blocks = rows // block
    split = width * 9 // 16
    fetch_q = pltpu.make_async_copy(q_hbm, q_ref, small_sems.at[0])
    fetch_groups = pltpu.make_async_copy(groups_hbm, groups_ref, small_sems.at[1])
    fetch_bias = pltpu.make_async_copy(bias_hbm, bias_ref, small_sems.at[2])
    fetch_q.start(priority=1)

    def fetches(b):
        at = pl.ds(b * block, block)
        return (
            pltpu.make_async_copy(grads_hbm.at[at], grads_ref.at[at], sems.at[0, b]),
            pltpu.make_async_copy(errors_hbm.at[at], errors_ref.at[at], sems.at[1, b]),
        )

    for b in range(blocks):
        for queue, copy in enumerate(fetches(b)):
            copy.start(priority=queue)
    fetch_groups.start(priority=0)
    fetch_bias.start(priority=1)
    fetch_q.wait()
    step = split // 3
    for k in range(0, split, step):
        q16_ref[:, k : k + step] = stack16(q_ref[:, k : k + step])
    for r in range(RANK):
        wide_q[r] = jnp.broadcast_to(q_ref[r : r + 1, split:], (8, width - split))

    def pool_bias():
        heads = groups_ref.shape[1]
        local_heads = bias_ref.shape[0]
        first = lax.axis_index("tensor") * local_heads
        head = lax.broadcasted_iota(jnp.int32, (NG, heads), 1)
        member = groups_ref[...] == lax.broadcasted_iota(jnp.int32, (NG, heads), 0)
        count = jnp.sum(jnp.where(member, 1.0, 0.0), axis=1, keepdims=True)
        mine = jnp.where(member & (head >= first) & (head < first + local_heads), 1.0, 0.0).astype(BF16)
        rows_of_all = jnp.concatenate([bias_ref[...]] * (heads // local_heads), axis=0)
        pooled = sum(jnp.dot(mine, piece.astype(BF16), preferred_element_type=F32) for piece in reversed(split3(rows_of_all)))
        bias_out[...] = pooled / (count * replicas)

    lane = lax.broadcasted_iota(jnp.int32, (strip, LANES), 1)

    def add_block(b):
        for start in range(b * block, (b + 1) * block, strip):
            at = slice(start, start + strip)
            sums = [jnp.zeros((strip // 8, 8, LANES), F32)] * RANK
            for k in range(split, width, LANES):
                merged = grads_ref[at, k : k + LANES].astype(F32) + errors_ref[at, k : k + LANES].astype(F32)
                merged = merged.reshape(strip // 8, 8, LANES)
                q_at = slice(k - split, k - split + LANES)
                sums = [sums[r] + merged * wide_q[r, :, q_at][None] for r in range(RANK)]
            columns = jnp.zeros((strip, LANES), F32)
            for r in range(RANK):
                column = jnp.sum(sums[r].reshape(strip, LANES), axis=1, keepdims=True)
                columns = jnp.where(lane == r, column, columns)
            sums_ref[at, :] = columns

    def product(b):
        at = slice(b * block, (b + 1) * block)
        terms = [
            lax.dot_general(q16_ref[...], held[at, 0:split], (((1,), (1,)), ((), ())), preferred_element_type=F32)
            for held in (grads_ref, errors_ref)
        ]
        return fold16(terms[0] + terms[1])

    terms = []
    for b in range(blocks):
        for copy in fetches(b):
            copy.wait()
        if b == blocks - 1:
            fetch_groups.wait()
            fetch_bias.wait()
            pool_bias()
        terms.append(product(b))
        add_block(b)
    left = jnp.concatenate(terms, axis=1) + sums_ref[...].T[0:RANK]
    left_ref[...] = jnp.broadcast_to(left[None], left_ref.shape)


def right_kernel(chunk, shards, replicas, bias_ref, left_terms, grads_ref, errors_ref, left_out, send_ref):
    n = send_ref.shape[0]
    width = grads_ref.shape[1]
    left = butterfly_sum([left_terms[r] for r in range(left_terms.shape[0])]) / replicas
    left_out[...] = left
    left16 = stack16(left)

    sub = lax.broadcasted_iota(jnp.int32, (RANK, LANES), 0)
    lane = lax.broadcasted_iota(jnp.int32, (RANK, LANES), 1)
    spread = jnp.zeros((RANK, LANES), F32)
    for i in range(RANK):
        column = jnp.sum(left * left[i : i + 1], axis=1, keepdims=True)
        spread += jnp.where(lane == RANK * i + sub, column, 0.0)
    gram_row = jnp.sum(spread, axis=0, keepdims=True)

    pieces = chunk // LANES
    bias_rows = NG // shards
    used = RANK * pieces
    per_step = max(1, 1536 // chunk)
    for start in range(0, n, per_step):
        cols = slice(start * chunk, min((start + per_step) * chunk, width))
        if cols.start < width:
            y16 = jnp.dot(left16, grads_ref[:, cols], preferred_element_type=F32)
            y16 += jnp.dot(left16, errors_ref[:, cols], preferred_element_type=F32)
            y = fold16(y16)
        for j in range(start, min(start + per_step, n)):
            for k in range(pieces):
                at = (j - start) * chunk + k * LANES
                if j * chunk < width:
                    send_ref[j, RANK * k : RANK * (k + 1), :] = y[:, at : at + LANES]
                else:
                    send_ref[j, RANK * k : RANK * (k + 1), :] = jnp.zeros((RANK, LANES), F32)
            group = (j % shards) * bias_rows
            send_ref[j, used : used + bias_rows, :] = bias_ref[group : group + bias_rows, :]
            send_ref[j, used + bias_rows : used + bias_rows + 1, :] = gram_row


def solve_kernel(chunk, bias_rows, replicas, left_ref, got_ref, p_ref, q_ref, bias_ref):
    n = got_ref.shape[0]
    copies = q_ref.shape[0]
    pieces = chunk // LANES
    used = RANK * pieces
    total = butterfly_sum([got_ref[j] for j in range(n)])
    bias_ref[...] = total[used : used + bias_rows]
    gram_row = total[used + bias_rows : used + bias_rows + 1] / replicas
    lane = lax.broadcasted_iota(jnp.int32, (1, LANES), 1)

    def entry(i, j):
        return jnp.sum(jnp.where(lane == RANK * i + j, gram_row, 0.0), axis=1, keepdims=True)

    chol = {}
    for j in range(RANK):
        for i in range(j, RANK):
            value = entry(i, j)
            for k in range(j):
                value = value - chol[i, k] * chol[j, k]
            chol[i, j] = jnp.sqrt(value) if i == j else value / chol[j, j]

    def forward(rows):
        solved = []
        for i in range(RANK):
            row = rows[i]
            for k in range(i):
                row = row - chol[i, k] * solved[k]
            solved.append(row / chol[i, i])
        return solved

    left = left_ref[...]
    for i, row in enumerate(forward([left[i : i + 1] for i in range(RANK)])):
        p_ref[i : i + 1, :] = row
    for k in range(pieces):
        part = total[RANK * k : RANK * (k + 1)] / replicas
        for i, row in enumerate(forward([part[i : i + 1] for i in range(RANK)])):
            q_ref[:, i : i + 1, k * LANES : (k + 1) * LANES] = jnp.broadcast_to(row[None], (copies, 1, LANES))


def errors_kernel(chunk, block, p_ref, bias_ref, q_chunks, grads_ref, errors_ref, out_hbm, p_hbm, q_hbm, bias_hbm, q_ref, q32_ref, out_ref, small_sems, sems):
    rows, width = grads_ref.shape
    copies = [
        pltpu.make_async_copy(p_ref, p_hbm, small_sems.at[0]),
        pltpu.make_async_copy(bias_ref, bias_hbm, small_sems.at[1]),
    ]
    for copy in copies:
        copy.start()
    p_high, p_mid, p_low = split3(p_ref[...])
    zero = jnp.zeros_like(p_high)
    p32 = jnp.concatenate([p_high, p_high, p_mid, p_high, p_low, p_mid, zero, zero], axis=0).T.astype(BF16)
    for j in range(width // chunk):
        q = q_chunks[j]
        cols = slice(j * chunk, (j + 1) * chunk)
        q_ref[:, cols] = q
        q_high, q_mid, q_low = split3(q)
        none = jnp.zeros_like(q)
        q32_ref[:, cols] = jnp.concatenate([q_high, q_mid, q_high, q_low, q_high, q_mid, none, none], axis=0).astype(BF16)
    copies.append(pltpu.make_async_copy(q_ref, q_hbm, small_sems.at[2]))
    copies[-1].start()
    step = width // 8
    for b in range(rows // block):
        at = slice(b * block, (b + 1) * block)
        for s in range(width // step):
            cols = slice(s * step, (s + 1) * step)
            approx = jnp.dot(p32[at], q32_ref[:, cols], preferred_element_type=F32)
            merged = grads_ref[at, cols].astype(F32) + errors_ref[at, cols].astype(F32)
            out_ref[at, cols] = (merged - approx).astype(BF16)
        to = pl.ds(b * block, block)
        copy = pltpu.make_async_copy(out_ref.at[to], out_hbm.at[to], sems.at[b])
        copy.start(priority=b % 2)
        copies.append(copy)
    for copy in copies:
        copy.wait()


def per_device(grads, errors, q_init, bias_grads, head_group):
    replicas, shards = lax.axis_size("dp"), lax.axis_size("tensor")
    n = replicas * shards
    _, rows, width = grads.shape
    chunk = LANES * math.ceil(width / (LANES * n))
    bias_rows = NG // shards
    send_rows = 8 * math.ceil((RANK * chunk // LANES + bias_rows + 1) / 8)
    vmem = pl.BlockSpec(memory_space=pltpu.VMEM)
    smem = pl.BlockSpec(memory_space=pltpu.SMEM)
    anywhere = pl.BlockSpec(memory_space=pl.ANY)
    block = 32

    held = pltpu.VMEM((rows, width), BF16)
    left, bias, held_grads, held_errors = pl.pallas_call(
        functools.partial(left_kernel, rows // 4, float(replicas)),
        out_shape=(pltpu.VMEM((replicas, RANK, rows), F32), pltpu.VMEM((NG, HD), F32), held, held),
        in_specs=[anywhere] * 5,
        out_specs=[vmem] * 4,
        scratch_shapes=[
            pltpu.VMEM((1, head_group.shape[0]), jnp.int32),
            pltpu.VMEM((RANK, width), F32),
            pltpu.VMEM((16, width * 9 // 16), BF16),
            pltpu.VMEM((RANK, 8, width - width * 9 // 16), F32),
            pltpu.VMEM((bias_grads.shape[1] // HD, HD), F32),
            pltpu.VMEM((rows, LANES), F32),
            pltpu.SemaphoreType.DMA((3,)),
            pltpu.SemaphoreType.DMA((2, 4)),
        ],
        compiler_params=pltpu.CompilerParams(vmem_limit_bytes=8 * MIB),
        name="left_term",
    )(*(pltpu.with_memory_space_constraint(x, pltpu.HBM) for x in (head_group.reshape(1, -1), q_init, bias_grads.reshape(-1, HD), grads[0], errors[0])))
    left_terms = lax.all_to_all(left, "dp", 0, 0, tiled=True)

    left, send = pl.pallas_call(
        functools.partial(right_kernel, chunk, shards, float(replicas)),
        out_shape=(jax.ShapeDtypeStruct((RANK, rows), F32), jax.ShapeDtypeStruct((n, send_rows, LANES), F32)),
        in_specs=[vmem] * 4,
        out_specs=[vmem] * 2,
        compiler_params=pltpu.CompilerParams(vmem_limit_bytes=16 * MIB),
        name="right_term",
    )(bias, left_terms, held_grads, held_errors)
    got = lax.all_to_all(send, ("dp", "tensor"), 0, 0, tiled=True)

    p, q_send, bias = pl.pallas_call(
        functools.partial(solve_kernel, chunk, bias_rows, float(replicas)),
        out_shape=(
            jax.ShapeDtypeStruct((RANK, rows), F32),
            jax.ShapeDtypeStruct((n, RANK, chunk), F32),
            jax.ShapeDtypeStruct((bias_rows, HD), F32),
        ),
        in_specs=[vmem] * 2,
        out_specs=[vmem] * 3,
        compiler_params=pltpu.CompilerParams(vmem_limit_bytes=16 * MIB),
        name="solve",
    )(left, got)
    q_chunks = lax.all_to_all(q_send, ("dp", "tensor"), 0, 0, tiled=True)

    new_errors, p_factor, q_factor, bias_update = pl.pallas_call(
        functools.partial(errors_kernel, chunk, block),
        out_shape=(
            jax.ShapeDtypeStruct((rows, width), BF16),
            jax.ShapeDtypeStruct((RANK, rows), F32),
            jax.ShapeDtypeStruct((RANK, width), F32),
            jax.ShapeDtypeStruct((bias_rows, HD), F32),
        ),
        in_specs=[vmem] * 5,
        out_specs=[anywhere] * 4,
        scratch_shapes=[
            pltpu.VMEM((RANK, width), F32),
            pltpu.VMEM((32, width), BF16),
            pltpu.VMEM((rows, width), BF16),
            pltpu.SemaphoreType.DMA((3,)),
            pltpu.SemaphoreType.DMA((rows // block,)),
        ],
        compiler_params=pltpu.CompilerParams(vmem_limit_bytes=24 * MIB),
        name="new_errors",
    )(p, bias, q_chunks, held_grads, held_errors)
    return (new_errors[None], p_factor, q_factor, bias_update.reshape(-1))


def solution(mesh):
    placed = (P("dp", "tensor", None), P("dp", "tensor", None), P(), P("dp", "tensor"), P())
    return jax.shard_map(
        per_device,
        mesh=mesh,
        in_specs=placed,
        out_specs=(P("dp", "tensor", None), P(None, "tensor"), P(), P("tensor")),
        check_vma=False,
    )
```

```python
import functools
import math

import jax
import jax.numpy as jnp
from jax import lax
from jax.experimental import pallas as pl
from jax.experimental.pallas import tpu as pltpu
from jax.sharding import PartitionSpec as P

HD = 128
NG = 8
RANK = 4
LANES = 128
MIB = 1 << 20
F32 = jnp.float32
BF16 = jnp.bfloat16


def split3(x):
    high = x.astype(BF16).astype(F32)
    rest = x - high
    mid = rest.astype(BF16).astype(F32)
    return high, mid, rest - mid


def stack16(x):
    high, mid, low = split3(x)
    return jnp.concatenate([high, mid, low, jnp.zeros_like(x)], axis=0).astype(BF16)


def fold16(x):
    return (x[8:12] + x[4:8]) + x[0:4]


def butterfly_sum(parts):
    while len(parts) > 1:
        parts = [parts[i] + parts[i + 1] for i in range(0, len(parts), 2)]
    return parts[0]


def left_kernel(replicas, groups_hbm, q_hbm, bias_hbm, grads_hbm, errors_hbm, left_ref, bias_out, grads_ref, errors_ref, groups_ref, q_ref, q16_ref, wide_q, bias_ref, sums_ref, small_sems, sems):
    rows, width = grads_hbm.shape
    strip = 32
    edges = [0, rows * 3 // 8 // strip * strip, rows * 3 // 4 // strip * strip, rows]
    blocks = [slice(i, j) for i, j in zip(edges, edges[1:])]
    split = width * 9 // 16
    fetch_q = pltpu.make_async_copy(q_hbm, q_ref, small_sems.at[0])
    fetch_groups = pltpu.make_async_copy(groups_hbm, groups_ref, small_sems.at[1])
    fetch_bias = pltpu.make_async_copy(bias_hbm, bias_ref, small_sems.at[2])
    fetch_q.start(priority=1)

    def fetches(b):
        at = pl.ds(blocks[b].start, blocks[b].stop - blocks[b].start)
        return (
            pltpu.make_async_copy(grads_hbm.at[at], grads_ref.at[at], sems.at[0, b]),
            pltpu.make_async_copy(errors_hbm.at[at], errors_ref.at[at], sems.at[1, b]),
        )

    for b in range(len(blocks)):
        for queue, copy in enumerate(fetches(b)):
            copy.start(priority=queue)
    fetch_groups.start(priority=0)
    fetch_bias.start(priority=1)
    fetch_q.wait()
    step = split // 3
    for k in range(0, split, step):
        q16_ref[:, k : k + step] = stack16(q_ref[:, k : k + step])
    for r in range(RANK):
        wide_q[r] = jnp.broadcast_to(q_ref[r : r + 1, split:], (8, width - split))

    def pool_bias():
        heads = groups_ref.shape[1]
        local_heads = bias_ref.shape[0]
        first = lax.axis_index("tensor") * local_heads
        head = lax.broadcasted_iota(jnp.int32, (NG, heads), 1)
        member = groups_ref[...] == lax.broadcasted_iota(jnp.int32, (NG, heads), 0)
        count = jnp.sum(jnp.where(member, 1.0, 0.0), axis=1, keepdims=True)
        mine = jnp.where(member & (head >= first) & (head < first + local_heads), 1.0, 0.0).astype(BF16)
        rows_of_all = jnp.concatenate([bias_ref[...]] * (heads // local_heads), axis=0)
        pooled = sum(jnp.dot(mine, piece.astype(BF16), preferred_element_type=F32) for piece in reversed(split3(rows_of_all)))
        bias_out[...] = pooled / (count * replicas)

    lane = lax.broadcasted_iota(jnp.int32, (strip, LANES), 1)

    def add_block(b):
        for start in range(blocks[b].start, blocks[b].stop, strip):
            at = slice(start, start + strip)
            sums = [jnp.zeros((strip // 8, 8, LANES), F32)] * RANK
            for k in range(split, width, LANES):
                merged = grads_ref[at, k : k + LANES].astype(F32) + errors_ref[at, k : k + LANES].astype(F32)
                merged = merged.reshape(strip // 8, 8, LANES)
                q_at = slice(k - split, k - split + LANES)
                sums = [sums[r] + merged * wide_q[r, :, q_at][None] for r in range(RANK)]
            columns = jnp.zeros((strip, LANES), F32)
            for r in range(RANK):
                column = jnp.sum(sums[r].reshape(strip, LANES), axis=1, keepdims=True)
                columns = jnp.where(lane == r, column, columns)
            sums_ref[at, :] = columns

    def product(b):
        at = blocks[b]
        terms = [
            lax.dot_general(q16_ref[...], held[at, 0:split], (((1,), (1,)), ((), ())), preferred_element_type=F32)
            for held in (grads_ref, errors_ref)
        ]
        return fold16(terms[0] + terms[1])

    terms = []
    for b in range(len(blocks)):
        for copy in fetches(b):
            copy.wait()
        if b == len(blocks) - 1:
            fetch_groups.wait()
            fetch_bias.wait()
            pool_bias()
        terms.append(product(b))
        add_block(b)
    left = jnp.concatenate(terms, axis=1) + sums_ref[...].T[0:RANK]
    left_ref[...] = jnp.broadcast_to(left[None], left_ref.shape)


def right_kernel(chunk, shards, replicas, bias_ref, left_terms, grads_ref, errors_ref, left_out, send_ref):
    n = send_ref.shape[0]
    width = grads_ref.shape[1]
    left = butterfly_sum([left_terms[r] for r in range(left_terms.shape[0])]) / replicas
    left_out[...] = left
    left16 = stack16(left)

    sub = lax.broadcasted_iota(jnp.int32, (RANK, LANES), 0)
    lane = lax.broadcasted_iota(jnp.int32, (RANK, LANES), 1)
    spread = jnp.zeros((RANK, LANES), F32)
    for i in range(RANK):
        column = jnp.sum(left * left[i : i + 1], axis=1, keepdims=True)
        spread += jnp.where(lane == RANK * i + sub, column, 0.0)
    gram_row = jnp.sum(spread, axis=0, keepdims=True)

    pieces = chunk // LANES
    bias_rows = NG // shards
    used = RANK * pieces
    per_step = max(1, 1536 // chunk)
    for start in range(0, n, per_step):
        cols = slice(start * chunk, min((start + per_step) * chunk, width))
        if cols.start < width:
            y16 = jnp.dot(left16, grads_ref[:, cols], preferred_element_type=F32)
            y16 += jnp.dot(left16, errors_ref[:, cols], preferred_element_type=F32)
            y = fold16(y16)
        for j in range(start, min(start + per_step, n)):
            for k in range(pieces):
                at = (j - start) * chunk + k * LANES
                if j * chunk < width:
                    send_ref[j, RANK * k : RANK * (k + 1), :] = y[:, at : at + LANES]
                else:
                    send_ref[j, RANK * k : RANK * (k + 1), :] = jnp.zeros((RANK, LANES), F32)
            group = (j % shards) * bias_rows
            send_ref[j, used : used + bias_rows, :] = bias_ref[group : group + bias_rows, :]
            send_ref[j, used + bias_rows : used + bias_rows + 1, :] = gram_row


def solve_kernel(chunk, bias_rows, replicas, left_ref, got_ref, p_ref, q_ref, bias_ref):
    n = got_ref.shape[0]
    copies = q_ref.shape[0]
    pieces = chunk // LANES
    used = RANK * pieces
    total = butterfly_sum([got_ref[j] for j in range(n)])
    bias_ref[...] = total[used : used + bias_rows]
    gram_row = total[used + bias_rows : used + bias_rows + 1] / replicas
    lane = lax.broadcasted_iota(jnp.int32, (1, LANES), 1)

    def entry(i, j):
        return jnp.sum(jnp.where(lane == RANK * i + j, gram_row, 0.0), axis=1, keepdims=True)

    chol = {}
    for j in range(RANK):
        for i in range(j, RANK):
            value = entry(i, j)
            for k in range(j):
                value = value - chol[i, k] * chol[j, k]
            chol[i, j] = jnp.sqrt(value) if i == j else value / chol[j, j]

    def forward(rows):
        solved = []
        for i in range(RANK):
            row = rows[i]
            for k in range(i):
                row = row - chol[i, k] * solved[k]
            solved.append(row / chol[i, i])
        return solved

    left = left_ref[...]
    for i, row in enumerate(forward([left[i : i + 1] for i in range(RANK)])):
        p_ref[i : i + 1, :] = row
    for k in range(pieces):
        part = total[RANK * k : RANK * (k + 1)] / replicas
        for i, row in enumerate(forward([part[i : i + 1] for i in range(RANK)])):
            q_ref[:, i : i + 1, k * LANES : (k + 1) * LANES] = jnp.broadcast_to(row[None], (copies, 1, LANES))


def errors_kernel(chunk, block, p_ref, bias_ref, q_chunks, grads_ref, errors_ref, out_hbm, p_hbm, q_hbm, bias_hbm, q_ref, q32_ref, out_ref, small_sems, sems):
    rows, width = grads_ref.shape
    copies = [
        pltpu.make_async_copy(p_ref, p_hbm, small_sems.at[0]),
        pltpu.make_async_copy(bias_ref, bias_hbm, small_sems.at[1]),
    ]
    for copy in copies:
        copy.start()
    p_high, p_mid, p_low = split3(p_ref[...])
    zero = jnp.zeros_like(p_high)
    p32 = jnp.concatenate([p_high, p_high, p_mid, p_high, p_low, p_mid, zero, zero], axis=0).T.astype(BF16)
    for j in range(width // chunk):
        q = q_chunks[j]
        cols = slice(j * chunk, (j + 1) * chunk)
        q_ref[:, cols] = q
        q_high, q_mid, q_low = split3(q)
        none = jnp.zeros_like(q)
        q32_ref[:, cols] = jnp.concatenate([q_high, q_mid, q_high, q_low, q_high, q_mid, none, none], axis=0).astype(BF16)
    copies.append(pltpu.make_async_copy(q_ref, q_hbm, small_sems.at[2]))
    copies[-1].start()
    step = width // 8
    for b in range(rows // block):
        at = slice(b * block, (b + 1) * block)
        for s in range(width // step):
            cols = slice(s * step, (s + 1) * step)
            approx = jnp.dot(p32[at], q32_ref[:, cols], preferred_element_type=F32)
            merged = grads_ref[at, cols].astype(F32) + errors_ref[at, cols].astype(F32)
            out_ref[at, cols] = (merged - approx).astype(BF16)
        to = pl.ds(b * block, block)
        copy = pltpu.make_async_copy(out_ref.at[to], out_hbm.at[to], sems.at[b])
        copy.start(priority=b % 2)
        copies.append(copy)
    for copy in copies:
        copy.wait()


def per_device(grads, errors, q_init, bias_grads, head_group):
    replicas, shards = lax.axis_size("dp"), lax.axis_size("tensor")
    n = replicas * shards
    _, rows, width = grads.shape
    chunk = LANES * math.ceil(width / (LANES * n))
    bias_rows = NG // shards
    send_rows = 8 * math.ceil((RANK * chunk // LANES + bias_rows + 1) / 8)
    vmem = pl.BlockSpec(memory_space=pltpu.VMEM)
    smem = pl.BlockSpec(memory_space=pltpu.SMEM)
    anywhere = pl.BlockSpec(memory_space=pl.ANY)
    block = 32

    held = pltpu.VMEM((rows, width), BF16)
    left, bias, held_grads, held_errors = pl.pallas_call(
        functools.partial(left_kernel, float(replicas)),
        out_shape=(pltpu.VMEM((replicas, RANK, rows), F32), pltpu.VMEM((NG, HD), F32), held, held),
        in_specs=[anywhere] * 5,
        out_specs=[vmem] * 4,
        scratch_shapes=[
            pltpu.VMEM((1, head_group.shape[0]), jnp.int32),
            pltpu.VMEM((RANK, width), F32),
            pltpu.VMEM((16, width * 9 // 16), BF16),
            pltpu.VMEM((RANK, 8, width - width * 9 // 16), F32),
            pltpu.VMEM((bias_grads.shape[1] // HD, HD), F32),
            pltpu.VMEM((rows, LANES), F32),
            pltpu.SemaphoreType.DMA((3,)),
            pltpu.SemaphoreType.DMA((2, 3)),
        ],
        compiler_params=pltpu.CompilerParams(vmem_limit_bytes=8 * MIB),
        name="left_term",
    )(*(pltpu.with_memory_space_constraint(x, pltpu.HBM) for x in (head_group.reshape(1, -1), q_init, bias_grads.reshape(-1, HD), grads[0], errors[0])))
    left_terms = lax.all_to_all(left, "dp", 0, 0, tiled=True)

    left, send = pl.pallas_call(
        functools.partial(right_kernel, chunk, shards, float(replicas)),
        out_shape=(jax.ShapeDtypeStruct((RANK, rows), F32), jax.ShapeDtypeStruct((n, send_rows, LANES), F32)),
        in_specs=[vmem] * 4,
        out_specs=[vmem] * 2,
        compiler_params=pltpu.CompilerParams(vmem_limit_bytes=16 * MIB),
        name="right_term",
    )(bias, left_terms, held_grads, held_errors)
    got = lax.all_to_all(send, ("dp", "tensor"), 0, 0, tiled=True)

    p, q_send, bias = pl.pallas_call(
        functools.partial(solve_kernel, chunk, bias_rows, float(replicas)),
        out_shape=(
            jax.ShapeDtypeStruct((RANK, rows), F32),
            jax.ShapeDtypeStruct((n, RANK, chunk), F32),
            jax.ShapeDtypeStruct((bias_rows, HD), F32),
        ),
        in_specs=[vmem] * 2,
        out_specs=[vmem] * 3,
        compiler_params=pltpu.CompilerParams(vmem_limit_bytes=16 * MIB),
        name="solve",
    )(left, got)
    q_chunks = lax.all_to_all(q_send, ("dp", "tensor"), 0, 0, tiled=True)

    new_errors, p_factor, q_factor, bias_update = pl.pallas_call(
        functools.partial(errors_kernel, chunk, block),
        out_shape=(
            jax.ShapeDtypeStruct((rows, width), BF16),
            jax.ShapeDtypeStruct((RANK, rows), F32),
            jax.ShapeDtypeStruct((RANK, width), F32),
            jax.ShapeDtypeStruct((bias_rows, HD), F32),
        ),
        in_specs=[vmem] * 5,
        out_specs=[anywhere] * 4,
        scratch_shapes=[
            pltpu.VMEM((RANK, width), F32),
            pltpu.VMEM((32, width), BF16),
            pltpu.VMEM((rows, width), BF16),
            pltpu.SemaphoreType.DMA((3,)),
            pltpu.SemaphoreType.DMA((rows // block,)),
        ],
        compiler_params=pltpu.CompilerParams(vmem_limit_bytes=24 * MIB),
        name="new_errors",
    )(p, bias, q_chunks, held_grads, held_errors)
    return (new_errors[None], p_factor, q_factor, bias_update.reshape(-1))


def solution(mesh):
    placed = (P("dp", "tensor", None), P("dp", "tensor", None), P(), P("dp", "tensor"), P())
    return jax.shard_map(
        per_device,
        mesh=mesh,
        in_specs=placed,
        out_specs=(P("dp", "tensor", None), P(None, "tensor"), P(), P("tensor")),
        check_vma=False,
    )
```
